32 devices in a mesh: member: 2 (over x), lon: 16 (over z, y, core).
Axes of the slice: x: 2, y: 2, z: 4, core: 2. Of those that a mesh axis runs over, the one named last changes fastest.
Arguments:
- obs_departure: bfloat16 [8192], P(('member', 'lon')), parts along dimension 0, may hold values from -6 to 6
- obs_precision: bfloat16 [4096], P('lon'), may hold values from 0.25 to 4
- obs_columns: int32 [4096], P('lon'), may hold values from 0 to 8191, as said below
- obs_counts: int32 [16], P('lon'), may hold values from 128 to 256, as said below
- obs_blocks: int32 [4096], P('lon'), may hold values from 0 to 63
- weight_table: bfloat16 [1024, 192], P('lon'), may hold values from -0.4375 to 0.4375
- lon_coeff: float32 [32, 64, 128], P(None, 'lon'), may hold values from 0.02 to 0.12
- lat_coeff: float32 [32, 64, 128], P(None, 'lon'), may hold values from 0.02 to 0.12
- vert_coeff: float32 [32, 64, 128], P(None, 'lon'), may hold values from 0.5 to 20
Outputs:
- control: float32 [12, 32, 64, 128], P('member', None, 'lon'), parts along dimension 0
- increment: float32 [12, 32, 64, 128], P('member', None, 'lon'), parts along dimension 0
- obs_fit: float32 [8192], P(('member', 'lon')), parts along dimension 0
The draws below stay inside these ranges and needn't reach their ends.
There are 2 independent parts, one for each index of `member`. The reference program is written for one: setup_inputs(seed, part) draws one part's arguments, and reference() takes and returns one part's arrays. A program takes and returns all parts, laid end to end along the dimension named above; an argument that names none is the same for every part. Nothing has to cross between parts.
Inputs may be any that keep to these rules, and one draw needn't show every extreme that they name: `obs_columns`: only live slots are read; dead slots hold valid column numbers. The live observations of one device put at most 32 into the columns of any one device (a block of 4 longitudes), and in every draw one device takes exactly 32 from every device. The live slots of a device are its first obs_counts ones; some device is full. `obs_blocks`: A row of the device's own part of weight_table.
All inputs are finite; a program needn't handle non-finite values.
Results may differ from the reference program's by a relative error of at most 0.0003.
Values may be sent and summed in bfloat16 or wider, within the bound.
A program may use at most 64 MiB of HBM per device.

```python
import math
import jax
import jax.numpy as jnp
from jax import lax

VARS = 6
LEV = 32
STEPS = 2
ITERS = 2
CLON = 4
NLAT = 128
OBS_DEV = 256
WB_DEV = 64
NLON = 64
OBS = 4096
N_LON = 16


def common_counts(key):
    first, second, third = jax.random.split(key, 3)
    counts = jax.random.randint(first, (N_LON,), OBS_DEV // 2, OBS_DEV + 1)
    full = jax.random.randint(second, (), 0, N_LON)
    lowest = (full + 1 + jax.random.randint(third, (), 0, N_LON - 1)) % N_LON
    places = jnp.arange(N_LON)
    counts = jnp.where(places == full, OBS_DEV, counts)
    counts = jnp.where(places == lowest, OBS_DEV // 2, counts)
    return counts.astype(jnp.int32)


def draw_obs_counts(key, part):
    counts = common_counts(key)
    return counts


def draw_obs_columns(key, part):
    counts = common_counts(key)
    key = jax.random.fold_in(key, 23)
    capacity = max(OBS_DEV // 64, 2 * ((OBS_DEV + N_LON - 1) // N_LON))
    key_hot, key_order, key_other, key_lon, key_lat = jax.random.split(key, 5)
    hottest = jax.random.randint(key_hot, (), 0, N_LON)
    slot_index = jnp.arange(OBS_DEV)
    live = (slot_index[None, :] < counts[:, None]).astype(jnp.int32)
    order = jax.vmap(lambda k: jax.random.permutation(k, OBS_DEV))(jax.random.split(key_order, N_LON))
    score = order + OBS_DEV * (1 - live)
    ranks = jnp.argsort(jnp.argsort(score, axis=1, stable=True), axis=1, stable=True)
    others = jax.vmap(lambda k: jax.random.permutation(k, N_LON - 1))(jax.random.split(key_other, N_LON))
    position = jnp.maximum(ranks - capacity, 0) % (N_LON - 1)
    other = jnp.take_along_axis(others, position, axis=1)
    other = other + (other >= hottest).astype(other.dtype)
    owner = jnp.where(ranks < capacity, hottest, other)
    lon_local = jax.random.randint(key_lon, (N_LON, OBS_DEV), 0, CLON)
    lat_local = jax.random.randint(key_lat, (N_LON, OBS_DEV), 0, NLAT)
    columns = (owner * CLON + lon_local) * NLAT + lat_local
    return columns.reshape(-1).astype(jnp.int32)


def with_ends(entries, rng, smallest, high):
    spot = [jax.random.randint(jax.random.fold_in(rng, axis), (), 0, length) for axis, length in enumerate(entries.shape)]
    longest = entries.shape.index(max(entries.shape))
    beside = spot[:longest] + [(spot[longest] + 1) % entries.shape[longest]] + spot[longest + 1:]
    return entries.at[tuple(spot)].set(smallest).at[tuple(beside)].set(high)


def level_of(stream_key, extent, pieces, least, largest):
    level, own = 1.0, jax.random.fold_in(stream_key, 6)
    for axis_at, shards_of in pieces:
        steps = jnp.exp(jax.random.uniform(jax.random.fold_in(own, axis_at), (shards_of,), jnp.float32, least / len(pieces), largest / len(pieces)))
        level = level * jnp.repeat(steps, extent[axis_at] // shards_of).reshape([-1 if axis == axis_at else 1 for axis in range(len(extent))])
    return level


def noise(rng, dims, scale, reach, cuts=(), held_as=jnp.bfloat16):
    result = jax.random.normal(rng, dims, jnp.float32) * scale
    if len(cuts) > 0:
        result = level_of(rng, dims, cuts, -0.22, 0.18) * result
    return jnp.clip(result, min=-reach, max=reach).astype(held_as)


def setup_inputs(seed: int = 0, part: int = 0) -> dict:
    key_of = jax.random.split(jax.random.key(seed), 10)
    own_keys = jax.random.split(jax.random.fold_in(key_of[9], part), 10)
    return {
        "obs_departure": noise(own_keys[0], (OBS,), 1.0, 6.0, ((0, 16),)),
        "obs_precision": jnp.clip(jnp.exp(math.log(4.0) - 2.7725887 * jax.random.uniform(key_of[1], (OBS,), jnp.float32) ** level_of(key_of[1], (OBS,), ((0, 16),), -0.2, 0.2)), 0.25, 4.0).astype(jnp.bfloat16),
        "obs_columns": draw_obs_columns(jax.random.fold_in(key_of[9], 71), part),
        "obs_counts": draw_obs_counts(jax.random.fold_in(key_of[9], 71), part),
        "obs_blocks": with_ends(jax.random.randint(key_of[4], (OBS,), 0, WB_DEV), jax.random.fold_in(key_of[4], 1), 0, WB_DEV - 1).astype(jnp.int32),
        "weight_table": noise(key_of[5], (N_LON * WB_DEV, VARS * LEV), (VARS * LEV) ** -0.5, 0.4375, ((0, 16),)),
        "lon_coeff": jnp.clip(jnp.exp(math.log(0.12) - 1.7917595 * jax.random.uniform(key_of[6], (LEV, NLON, NLAT), jnp.float32) ** level_of(key_of[6], (LEV, NLON, NLAT), ((1, 16),), -0.2, 0.2)), 0.02, 0.12),
        "lat_coeff": jnp.clip(jnp.exp(math.log(0.12) - 1.7917595 * jax.random.uniform(key_of[7], (LEV, NLON, NLAT), jnp.float32) ** level_of(key_of[7], (LEV, NLON, NLAT), ((1, 16),), -0.2, 0.2)), 0.02, 0.12),
        "vert_coeff": jnp.clip(jnp.exp(math.log(20.0) - 3.6888795 * jax.random.uniform(key_of[8], (LEV, NLON, NLAT), jnp.float32) ** level_of(key_of[8], (LEV, NLON, NLAT), ((1, 16),), -0.2, 0.2)), 0.5, 20.0),
    }


def level_lower(field, stride, fill):
    axis = field.ndim - 3
    widths = [(stride, 0) if i == axis else (0, 0) for i in range(field.ndim)]
    padded = jnp.pad(field, widths, constant_values=fill)
    return lax.slice_in_dim(padded, 0, field.shape[axis], axis=axis)


def level_upper(field, stride, fill):
    axis = field.ndim - 3
    widths = [(0, stride) if i == axis else (0, 0) for i in range(field.ndim)]
    padded = jnp.pad(field, widths, constant_values=fill)
    return lax.slice_in_dim(padded, stride, stride + field.shape[axis], axis=axis)


def factor_vertical(vert):
    levels = vert.shape[0]
    inner = (jnp.arange(levels) < levels - 1)[:, None, None]
    upward = jnp.where(inner, vert, jnp.zeros_like(vert))
    downward = level_lower(upward, 1, 0.0)
    lower = -downward
    diag = 1.0 + downward + upward
    upper = -upward
    factors = []
    stride = 1
    while stride < levels:
        alpha = -lower / level_lower(diag, stride, 1.0)
        gamma = -upper / level_upper(diag, stride, 1.0)
        new_lower = alpha * level_lower(lower, stride, 0.0)
        new_upper = gamma * level_upper(upper, stride, 0.0)
        diag = diag + alpha * level_lower(upper, stride, 0.0) + gamma * level_upper(lower, stride, 0.0)
        factors.append((stride, alpha, gamma))
        lower = new_lower
        upper = new_upper
        stride = stride * 2
    return factors, diag


def apply_vertical(factored, field):
    factors, diag = factored
    rhs = field
    for stride, alpha, gamma in factors:
        rhs = rhs + alpha * level_lower(rhs, stride, 0.0) + gamma * level_upper(rhs, stride, 0.0)
    return rhs / diag


def diffuse(field, along, across):
    nlat = field.shape[-1]
    open_face = jnp.arange(nlat) < nlat - 1
    flux_lon = along * (jnp.roll(field, -1, axis=-2) - field)
    flux_lat = jnp.where(open_face, across * (jnp.roll(field, -1, axis=-1) - field), 0.0)
    return field + flux_lon - jnp.roll(flux_lon, 1, axis=-2) + flux_lat - jnp.roll(flux_lat, 1, axis=-1)


def reference(obs_departure, obs_precision, obs_columns, obs_counts, obs_blocks, weight_table, lon_coeff, lat_coeff, vert_coeff):
    total = obs_columns.shape[0]
    devices = obs_counts.shape[0]
    per_dev = total // devices
    table_dev = weight_table.shape[0] // devices
    index = jnp.arange(total, dtype=jnp.int32)
    source = index // per_dev
    live = (index - source * per_dev) < obs_counts[source]
    rows = (source * table_dev + obs_blocks).astype(jnp.int32)
    block_weights = weight_table[rows].astype(jnp.float32)
    precision = jnp.where(live, obs_precision.astype(jnp.float32), 0.0)
    departure = obs_departure.astype(jnp.float32)
    state_shape = (VARS, LEV, lon_coeff.shape[1], lon_coeff.shape[2])
    ncols = lon_coeff.shape[1] * lon_coeff.shape[2]
    factored = factor_vertical(vert_coeff)

    def forward(field):
        flat = field.reshape(VARS * LEV, ncols)
        picked = jnp.take(flat, obs_columns, axis=1)
        return jnp.where(live, jnp.sum(block_weights * picked.T, axis=1), 0.0)

    def adjoint(values):
        contrib = block_weights * jnp.where(live, values, 0.0)[:, None]
        flat = jnp.zeros((ncols, VARS * LEV), jnp.float32).at[obs_columns].add(contrib)
        return flat.T.reshape(state_shape)

    def smooth(field):
        for step in range(STEPS):
            field = diffuse(field, lon_coeff, lat_coeff)
        return field

    def root(field):
        return apply_vertical(factored, smooth(field))

    def root_adjoint(field):
        return smooth(apply_vertical(factored, field))

    rhs = root_adjoint(adjoint(precision * departure))
    control = jnp.zeros(state_shape, jnp.float32)
    residual = rhs
    direction = rhs
    norm_now = jnp.sum(residual * residual)
    for step in range(ITERS):
        image = direction + root_adjoint(adjoint(precision * forward(root(direction))))
        alpha = norm_now / jnp.sum(direction * image)
        control = control + alpha * direction
        residual = residual - alpha * image
        fresh = jnp.sum(residual * residual)
        direction = residual + (fresh / norm_now) * direction
        norm_now = fresh
    increment = root(control)
    obs_fit = jnp.where(live, forward(increment) - departure, 0.0)
    return (control, increment, obs_fit)
```

```python
import jax
import jax.numpy as jnp
from jax import lax
from jax.sharding import PartitionSpec as P

VARS = 6
LEV = 32
STEPS = 2
EXACT = lax.Precision.HIGHEST


def neighbours(block, axis):
    count = lax.axis_size(axis)
    up = [(i, (i + 1) % count) for i in range(count)]
    down = [(target, source) for source, target in up]
    return lax.ppermute(block, axis, up), lax.ppermute(block, axis, down)


def shifted(field, stride, fill):
    widths = [(0, 0)] * field.ndim
    widths[-2] = (max(stride, 0), max(-stride, 0))
    padded = jnp.pad(field, widths, constant_values=fill)
    first = max(-stride, 0)
    return lax.slice_in_dim(padded, first, first + field.shape[-2], axis=field.ndim - 2)


def factor_vertical(vert):
    levels = vert.shape[-2]
    inner = (jnp.arange(levels) < levels - 1)[:, None]
    upward = jnp.where(inner, vert, 0.0)
    downward = shifted(upward, 1, 0.0)
    lower, upper = -downward, -upward
    diag = 1.0 + downward + upward
    factors = []
    stride = 1
    while stride < levels:
        alpha = -lower / shifted(diag, stride, 1.0)
        gamma = -upper / shifted(diag, -stride, 1.0)
        new_lower = alpha * shifted(lower, stride, 0.0)
        new_upper = gamma * shifted(upper, -stride, 0.0)
        diag = diag + alpha * shifted(upper, stride, 0.0) + gamma * shifted(lower, -stride, 0.0)
        factors.append((stride, alpha, gamma))
        lower, upper = new_lower, new_upper
        stride *= 2
    return factors, 1.0 / diag


def solve_vertical(factored, field, first, count):
    factors, scale = factored
    for stride, alpha, gamma in factors:
        alpha, gamma = alpha[first : first + count], gamma[first : first + count]
        field = field + alpha * shifted(field, stride, 0.0) + gamma * shifted(field, -stride, 0.0)
    return field * scale[first : first + count]


def smooth(field, along, across, first):
    for _ in range(STEPS):
        count = field.shape[1]
        flux_lon = along[first : first + count - 1] * (field[:, 1:] - field[:, :-1])
        middle = field[:, 1:-1]
        flux_lat = across[first + 1 : first + count - 1] * (jnp.roll(middle, -1, -1) - middle)
        field = middle + flux_lon[:, 1:] - flux_lon[:, :-1] + flux_lat - jnp.roll(flux_lat, 1, -1)
        first += 1
    return field


def on_device(
    obs_departure,
    obs_precision,
    obs_columns,
    obs_counts,
    obs_blocks,
    weight_table,
    lon_coeff,
    lat_coeff,
    vert_coeff,
):
    devices = lax.axis_size("lon")
    me = lax.axis_index("lon")
    levels, width, nlat = lon_coeff.shape
    percol = width * nlat
    depth = VARS * LEV
    per_dev = obs_columns.shape[0]
    capacity = max(per_dev // 64, 2 * ((per_dev + devices - 1) // devices))
    slots_all = devices * capacity
    bf16, f32 = jnp.bfloat16, jnp.float32

    open_face = jnp.arange(nlat) < nlat - 1
    coeffs = jnp.stack([lon_coeff, jnp.where(open_face, lat_coeff, 0.0), vert_coeff])
    coeffs = coeffs.transpose(0, 2, 1, 3)
    below, above = neighbours(coeffs, "lon")
    along, across, vert = jnp.concatenate([below, coeffs, above], axis=1)
    factored = factor_vertical(vert)

    slot = jnp.arange(per_dev, dtype=jnp.int32)
    live = slot < obs_counts[0]
    owner = obs_columns // percol
    local_col = obs_columns - owner * percol
    hits = (owner[:, None] == jnp.arange(devices, dtype=jnp.int32)) & live[:, None]
    before = jnp.dot(
        (slot[:, None] > slot).astype(bf16), hits.astype(bf16), preferred_element_type=f32
    )
    rank = jnp.sum(jnp.where(hits, before, 0.0), axis=1).astype(jnp.int32)
    target = jnp.where(live, owner * capacity + rank, slots_all)
    place = jnp.arange(slots_all, dtype=jnp.int32)[:, None] == target
    rows = weight_table.shape[0]
    pick = (obs_blocks[:, None] == jnp.arange(rows, dtype=jnp.int32)).astype(bf16)
    block_rows = jnp.dot(pick, weight_table, preferred_element_type=f32).astype(bf16)
    extra = jnp.stack(
        [
            obs_precision,
            obs_departure,
            (local_col // 16).astype(bf16),
            (local_col % 16).astype(bf16),
        ],
        axis=1,
    )
    payload = jnp.concatenate([block_rows, extra], axis=1)
    payload = jnp.dot(place.astype(bf16), payload, preferred_element_type=f32).astype(bf16)
    mine = lax.all_to_all(payload, "lon", split_axis=0, concat_axis=0, tiled=True)
    left, right = neighbours(mine, "lon")
    held = jnp.stack([left, mine, right])
    weights = held[..., :depth].astype(f32)
    precision = held[..., depth].astype(f32)
    departure = held[..., depth + 1].astype(f32)
    column = held[..., depth + 2].astype(jnp.int32) * 16 + held[..., depth + 3].astype(jnp.int32)
    at_column = column[..., None] == jnp.arange(percol, dtype=jnp.int32)
    own_precision = precision[1]

    def forward(field):
        flat = field.transpose(0, 2, 1, 3).reshape(depth, percol)
        dots = jnp.dot(weights[1], flat, precision=EXACT)
        return jnp.sum(jnp.where(at_column[1], dots, 0.0), axis=1)

    def adjoint(values):
        spread = jnp.where(at_column, values[..., None], 0.0)
        flat = jnp.einsum("bsc,bsn->cbn", weights, spread, precision=EXACT)
        return (
            flat.reshape(VARS, levels, 3 * width, nlat).transpose(0, 2, 1, 3)
        )

    def root(field):
        return solve_vertical(factored, smooth(field, along, across, STEPS), width, width)

    def root_adjoint(field):
        return smooth(solve_vertical(factored, field, 0, 3 * width), along, across, 0)

    def own(field):
        return field[:, STEPS : STEPS + width]

    rhs = root_adjoint(adjoint(precision * departure))
    rhs_own = own(rhs)
    rhs_root = root(rhs)
    rhs_obs = forward(rhs_root)
    weighted = own_precision * rhs_obs
    sums = jnp.stack([jnp.sum(rhs_own * rhs_own), jnp.sum(weighted * rhs_obs)])
    message = jnp.concatenate([weighted, sums])
    message = jnp.broadcast_to(message, (devices, slots_all + 2))
    message = lax.all_to_all(message, "lon", split_axis=0, concat_axis=0, tiled=True)
    norm, fit_norm = jnp.sum(message[:, slots_all:], axis=0)
    around = jnp.stack([(me + devices - 1) % devices, me, (me + 1) % devices])
    image = rhs + root_adjoint(adjoint(message[around, :slots_all]))
    alpha = norm / (norm + fit_norm)
    residual = rhs - alpha * image
    residual_own = own(residual)
    residual_root = root(residual)
    residual_obs = forward(residual_root)
    weighted = own_precision * residual_obs
    sums = jnp.stack(
        [
            jnp.sum(residual_own * residual_own),
            jnp.sum(residual_own * rhs_own),
            jnp.sum(weighted * residual_obs),
            jnp.sum(weighted * rhs_obs),
        ]
    )
    message = jnp.concatenate(
        [
            rhs_obs.reshape(devices, capacity),
            residual_obs.reshape(devices, capacity),
            jnp.broadcast_to(sums, (devices, 4)),
        ],
        axis=1,
    )
    message = lax.all_to_all(message, "lon", split_axis=0, concat_axis=0, tiled=True)
    fresh, cross, fit_fresh, fit_cross = jnp.sum(message[:, 2 * capacity :], axis=0)
    beta = fresh / norm
    curve = (
        fresh + fit_fresh + 2.0 * beta * (cross + fit_cross) + beta * beta * (norm + fit_norm)
    )
    second = fresh / curve
    first = alpha + second * beta
    control = first * rhs_own + second * residual_own
    increment = first * rhs_root + second * residual_root
    fit = first * message[:, :capacity] + second * message[:, capacity : 2 * capacity]
    fit = jnp.dot(fit.reshape(1, slots_all), place.astype(f32), precision=EXACT)[0]
    obs_fit = jnp.where(live, fit - obs_departure.astype(f32), 0.0)
    return control.transpose(0, 2, 1, 3), increment.transpose(0, 2, 1, 3), obs_fit


def solution(mesh):
    in_specs = (
        P(("member", "lon")),
        P("lon"),
        P("lon"),
        P("lon"),
        P("lon"),
        P("lon", None),
        P(None, "lon", None),
        P(None, "lon", None),
        P(None, "lon", None),
    )
    out_specs = (
        P("member", None, "lon", None),
        P("member", None, "lon", None),
        P(("member", "lon")),
    )
    return jax.shard_map(
        on_device, mesh=mesh, in_specs=in_specs, out_specs=out_specs, check_vma=False
    )
```

```python
import jax
import jax.numpy as jnp
from jax import lax
from jax.experimental import pallas as pl
from jax.experimental.pallas import tpu as pltpu
from jax.sharding import PartitionSpec as P

VARS = 6
LEV = 32
STEPS = 2
EXACT = lax.Precision.HIGHEST


def neighbours(block, axis):
    count = lax.axis_size(axis)
    up = [(i, (i + 1) % count) for i in range(count)]
    down = [(target, source) for source, target in up]
    return lax.ppermute(block, axis, up), lax.ppermute(block, axis, down)


def factor_vertical(vert):
    levels = vert.shape[-2]
    level = lax.broadcasted_iota(jnp.int32, vert.shape, vert.ndim - 2)
    axis = vert.ndim - 2
    upward = jnp.where(level < levels - 1, vert, 0.0)
    downward = jnp.where(level > 0, pltpu.roll(upward, 1, axis), 0.0)
    lower, upper = -downward, -upward
    diag = 1.0 + downward + upward
    factors = []
    stride = 1
    while stride < levels:
        back = levels - stride
        alpha = -lower / pltpu.roll(diag, stride, axis)
        gamma = -upper / pltpu.roll(diag, back, axis)
        new_lower = alpha * pltpu.roll(lower, stride, axis)
        new_upper = gamma * pltpu.roll(upper, back, axis)
        diag = diag + alpha * pltpu.roll(upper, stride, axis) + gamma * pltpu.roll(lower, back, axis)
        factors.append((alpha, gamma))
        lower, upper = new_lower, new_upper
        stride *= 2
    return factors, 1.0 / diag


def solve_vertical(alphas, gammas, scale, field, first):
    count, levels = field.shape[:2]
    held = pl.ds(first, count)
    for step in range(alphas.shape[0]):
        stride = 2**step
        field = (
            field
            + alphas[step, held] * pltpu.roll(field, stride, 1)
            + gammas[step, held] * pltpu.roll(field, levels - stride, 1)
        )
    return field * scale[held]


def smooth(along, across, field, first):
    nlat = field.shape[-1]
    for _ in range(STEPS):
        count = field.shape[0]
        flux_lon = along[pl.ds(first, count - 1)] * (field[1:] - field[:-1])
        middle = field[1:-1]
        flux_lat = across[pl.ds(first + 1, count - 2)] * (pltpu.roll(middle, nlat - 1, 2) - middle)
        field = middle + flux_lon[1:] - flux_lon[:-1] + flux_lat - pltpu.roll(flux_lat, 1, 2)
        first += 1
    return field


def thirds(value):
    parts = []
    for _ in range(3):
        part = value.astype(jnp.bfloat16)
        parts.append(part)
        value = value - part.astype(jnp.float32)
    return parts


def matmul(left, right, contract):
    return lax.dot_general(
        left, right, (contract, ((), ())), preferred_element_type=jnp.float32
    )


def hit_matrix(column, percol):
    cell = lax.broadcasted_iota(jnp.int32, (percol, column.shape[1]), 0).astype(jnp.float32)
    return jnp.where(cell == column, 1.0, 0.0).astype(jnp.bfloat16)


def adjoint(weights, hits, values, block):
    spread = weights[block].astype(jnp.float32) * values
    return sum(matmul(part, hits[block], ((1,), (1,))) for part in thirds(spread))


def forward(weights, hits, field):
    flat = jnp.concatenate([field[x] for x in range(field.shape[0])], axis=1)
    picked = sum(matmul(part, hits[1], ((1,), (0,))) for part in thirds(flat))
    return jnp.sum(weights[1].astype(jnp.float32) * picked, axis=0, keepdims=True)


def spread_out(values, weights, hits, field, width):
    for block in range(3):
        flat = adjoint(weights, hits, values[block], block)
        lanes = flat.shape[1] // width
        for x in range(width):
            field[block * width + x] = flat[:, x * lanes : (x + 1) * lanes]


def total(value, lanes):
    return jnp.full((1, lanes), jnp.sum(value), jnp.float32)


def first_kernel(
    coeffs_low, coeffs, coeffs_high, left, mine, right,
    rhs, root, weights, hits, along, across, alphas, gammas, scale, precision, message,
    field, norm,
):
    width, levels, nlat = coeffs.shape[1:]
    depth = weights.shape[1]
    for place, source in enumerate((coeffs_low, coeffs, coeffs_high)):
        held = pl.ds(place * width, width)
        along[held] = source[0]
        across[held] = source[1]
        factors, inverse = factor_vertical(source[2])
        scale[held] = inverse
        for step, (alpha, gamma) in enumerate(factors):
            alphas[step, held] = alpha
            gammas[step, held] = gamma
    start = []
    for block, source in enumerate((left, mine, right)):
        turned = source[...].astype(jnp.float32).T
        weights[block] = turned[:depth].astype(jnp.bfloat16)
        column = turned[depth + 2 : depth + 3] * 16.0 + turned[depth + 3 : depth + 4]
        hits[block] = hit_matrix(column, width * nlat)
        start.append(turned[depth : depth + 1] * turned[depth + 1 : depth + 2])
        if block == 1:
            precision[...] = turned[depth : depth + 1]
    spread_out(start, weights, hits, field, width)
    norm[...] = jnp.zeros_like(norm)

    def variable(index, carry):
        part = pl.ds(pl.multiple_of(index * levels, levels), levels)
        solved = solve_vertical(alphas, gammas, scale, field[:, part, :], 0)
        own = smooth(along, across, solved, 0)
        rhs[:, part, :] = own
        inner = own[STEPS : STEPS + width]
        norm[...] += jnp.sum(inner * inner, axis=0)
        root[:, part, :] = solve_vertical(
            alphas, gammas, scale, smooth(along, across, own, STEPS), width
        )
        return carry

    lax.fori_loop(0, VARS, variable, 0)
    seen = forward(weights, hits, root)
    weighted = precision[...] * seen
    slots = seen.shape[1]
    message[0:1, :] = weighted
    message[1:2, :] = seen
    message[2:3, :] = total(norm[...], slots)
    message[3:4, :] = total(weighted * seen, slots)
    message[4:8, :] = jnp.zeros((4, slots), jnp.float32)


def second_kernel(
    around, gathered, message, rhs, weights, hits, along, across, alphas, gammas, scale, precision,
    residual, root, sent,
    field, norm, cross,
):
    levels, nlat = scale.shape[1:]
    width = residual.shape[0]
    slots = precision.shape[1]
    values = [gathered[pl.ds(around[block], 1), 0:slots] for block in range(3)]
    spread_out(values, weights, hits, field, width)
    first = jnp.sum(gathered[:, slots : slots + nlat], axis=0, keepdims=True)
    fit = jnp.sum(gathered[:, slots + nlat : slots + 2 * nlat], axis=0, keepdims=True)
    alpha = (first / (first + fit))[None]
    norm[...] = jnp.zeros_like(norm)
    cross[...] = jnp.zeros_like(cross)

    def variable(index, carry):
        part = pl.ds(pl.multiple_of(index * levels, levels), levels)
        solved = solve_vertical(alphas, gammas, scale, field[:, part, :], 0)
        start = rhs[:, part, :]
        image = start + smooth(along, across, solved, 0)
        left = start - alpha * image
        inner = left[STEPS : STEPS + width]
        residual[:, part, :] = inner
        norm[...] += jnp.sum(inner * inner, axis=0)
        cross[...] += jnp.sum(inner * start[STEPS : STEPS + width], axis=0)
        root[:, part, :] = solve_vertical(
            alphas, gammas, scale, smooth(along, across, left, STEPS), width
        )
        return carry

    lax.fori_loop(0, VARS, variable, 0)
    seen = forward(weights, hits, root)
    weighted = precision[...] * seen
    sent[0:1, :] = seen
    sent[1:2, :] = total(norm[...], slots)
    sent[2:3, :] = total(cross[...], slots)
    sent[3:4, :] = total(weighted * seen, slots)
    sent[4:5, :] = total(weighted * message[1:2, :], slots)
    sent[5:8, :] = jnp.zeros((3, slots), jnp.float32)


def on_device(
    obs_departure,
    obs_precision,
    obs_columns,
    obs_counts,
    obs_blocks,
    weight_table,
    lon_coeff,
    lat_coeff,
    vert_coeff,
):
    devices = lax.axis_size("lon")
    me = lax.axis_index("lon")
    levels, width, nlat = lon_coeff.shape
    percol = width * nlat
    depth = VARS * LEV
    per_dev = obs_columns.shape[0]
    capacity = max(per_dev // 64, 2 * ((per_dev + devices - 1) // devices))
    slots_all = devices * capacity
    bf16, f32 = jnp.bfloat16, jnp.float32

    open_face = jnp.arange(nlat) < nlat - 1
    coeffs = jnp.stack([lon_coeff, jnp.where(open_face, lat_coeff, 0.0), vert_coeff])
    coeffs = coeffs.transpose(0, 2, 1, 3)
    below, above = neighbours(coeffs, "lon")

    slot = jnp.arange(per_dev, dtype=jnp.int32)
    live = slot < obs_counts[0]
    owner = obs_columns // percol
    local_col = obs_columns - owner * percol
    hits = (owner[:, None] == jnp.arange(devices, dtype=jnp.int32)) & live[:, None]
    before = jnp.dot(
        (slot[:, None] > slot).astype(bf16), hits.astype(bf16), preferred_element_type=f32
    )
    rank = jnp.sum(jnp.where(hits, before, 0.0), axis=1).astype(jnp.int32)
    target = jnp.where(live, owner * capacity + rank, slots_all)
    place = jnp.arange(slots_all, dtype=jnp.int32)[:, None] == target
    rows = weight_table.shape[0]
    pick = (obs_blocks[:, None] == jnp.arange(rows, dtype=jnp.int32)).astype(bf16)
    block_rows = jnp.dot(pick, weight_table, preferred_element_type=f32).astype(bf16)
    extra = jnp.stack(
        [
            obs_precision,
            obs_departure,
            (local_col // 16).astype(bf16),
            (local_col % 16).astype(bf16),
        ],
        axis=1,
    )
    lanes = -(-(depth + 4) // 128) * 128
    payload = jnp.concatenate([block_rows, extra], axis=1)
    payload = jnp.pad(payload, ((0, 0), (0, lanes - depth - 4)))
    payload = jnp.dot(place.astype(bf16), payload, preferred_element_type=f32).astype(bf16)
    mine = lax.all_to_all(payload, "lon", split_axis=0, concat_axis=0, tiled=True)
    left, right = neighbours(mine, "lon")
    wide = 3 * width
    middle = width + 2 * STEPS
    steps = (levels - 1).bit_length()
    vmem = pl.BlockSpec(memory_space=pltpu.VMEM)
    limit = pltpu.CompilerParams(vmem_limit_bytes=40 * 2**20)

    def shape(*dims, dtype=f32):
        return jax.ShapeDtypeStruct(dims, dtype)

    rhs, rhs_root, *held, message = pl.pallas_call(
        first_kernel,
        out_shape=[
            shape(middle, depth, nlat),
            shape(width, depth, nlat),
            shape(3, depth, slots_all, dtype=bf16),
            shape(3, percol, slots_all, dtype=bf16),
            shape(wide, levels, nlat),
            shape(wide, levels, nlat),
            shape(steps, wide, levels, nlat),
            shape(steps, wide, levels, nlat),
            shape(wide, levels, nlat),
            shape(1, slots_all),
            shape(8, slots_all),
        ],
        in_specs=[vmem] * 6,
        out_specs=[vmem] * 11,
        scratch_shapes=[pltpu.VMEM((wide, depth, nlat), f32), pltpu.VMEM((levels, nlat), f32)],
        compiler_params=limit,
    )(below, coeffs, above, left, mine, right)
    rhs_obs = message[1]
    gathered = jnp.concatenate([message[0], message[2, :nlat], message[3, :nlat]])
    gathered = jnp.broadcast_to(gathered, (devices, slots_all + 2 * nlat))
    gathered = lax.all_to_all(gathered, "lon", split_axis=0, concat_axis=0, tiled=True)
    norm = jnp.sum(gathered[:, slots_all])
    fit_norm = jnp.sum(gathered[:, slots_all + nlat])
    around = jnp.stack([(me + devices - 1) % devices, me, (me + 1) % devices])
    residual, residual_root, sent = pl.pallas_call(
        second_kernel,
        out_shape=[
            shape(width, depth, nlat),
            shape(width, depth, nlat),
            shape(8, slots_all),
        ],
        in_specs=[pl.BlockSpec(memory_space=pltpu.SMEM)] + [vmem] * 11,
        out_specs=[vmem] * 3,
        scratch_shapes=[pltpu.VMEM((wide, depth, nlat), f32)]
        + [pltpu.VMEM((levels, nlat), f32)] * 2,
        compiler_params=limit,
    )(around, gathered, message, rhs, *held)
    message = jnp.concatenate(
        [
            rhs_obs.reshape(devices, capacity),
            sent[0].reshape(devices, capacity),
            jnp.broadcast_to(sent[1:5, 0], (devices, 4)),
        ],
        axis=1,
    )
    message = lax.all_to_all(message, "lon", split_axis=0, concat_axis=0, tiled=True)
    fresh, cross, fit_fresh, fit_cross = jnp.sum(message[:, 2 * capacity :], axis=0)
    alpha = norm / (norm + fit_norm)
    beta = fresh / norm
    curve = (
        fresh + fit_fresh + 2.0 * beta * (cross + fit_cross) + beta * beta * (norm + fit_norm)
    )
    second = fresh / curve
    first = alpha + second * beta
    control = first * rhs[STEPS : STEPS + width] + second * residual
    increment = first * rhs_root + second * residual_root
    fit = first * message[:, :capacity] + second * message[:, capacity : 2 * capacity]
    fit = jnp.dot(fit.reshape(1, slots_all), place.astype(f32), precision=EXACT)[0]
    obs_fit = jnp.where(live, fit - obs_departure.astype(f32), 0.0)


    def placed(field):
        return field.reshape(width, VARS, levels, nlat).transpose(1, 2, 0, 3)

    return placed(control), placed(increment), obs_fit


def solution(mesh):
    in_specs = (
        P(("member", "lon")),
        P("lon"),
        P("lon"),
        P("lon"),
        P("lon"),
        P("lon", None),
        P(None, "lon", None),
        P(None, "lon", None),
        P(None, "lon", None),
    )
    out_specs = (
        P("member", None, "lon", None),
        P("member", None, "lon", None),
        P(("member", "lon")),
    )
    return jax.shard_map(
        on_device, mesh=mesh, in_specs=in_specs, out_specs=out_specs, check_vma=False
    )
```

```python
import jax
import jax.numpy as jnp
from jax import lax
from jax.experimental import pallas as pl
from jax.experimental.pallas import tpu as pltpu
from jax.sharding import PartitionSpec as P

VARS = 6
LEV = 32
STEPS = 2
EXACT = lax.Precision.HIGHEST


def factor_vertical(vert):
    levels = vert.shape[-2]
    level = lax.broadcasted_iota(jnp.int32, vert.shape, vert.ndim - 2)
    axis = vert.ndim - 2
    upward = jnp.where(level < levels - 1, vert, 0.0)
    downward = jnp.where(level > 0, pltpu.roll(upward, 1, axis), 0.0)
    lower, upper = -downward, -upward
    diag = 1.0 + downward + upward
    factors = []
    stride = 1
    while stride < levels:
        back = levels - stride
        alpha = -lower / pltpu.roll(diag, stride, axis)
        gamma = -upper / pltpu.roll(diag, back, axis)
        new_lower = alpha * pltpu.roll(lower, stride, axis)
        new_upper = gamma * pltpu.roll(upper, back, axis)
        diag = diag + alpha * pltpu.roll(upper, stride, axis) + gamma * pltpu.roll(lower, back, axis)
        factors.append((alpha, gamma))
        lower, upper = new_lower, new_upper
        stride *= 2
    return factors, 1.0 / diag


def solve_vertical(alphas, gammas, scale, field, first):
    count, levels = field.shape[:2]
    held = pl.ds(first, count)
    for step in range(alphas.shape[0]):
        stride = 2**step
        field = (
            field
            + alphas[step, held] * pltpu.roll(field, stride, 1)
            + gammas[step, held] * pltpu.roll(field, levels - stride, 1)
        )
    return field * scale[held]


def smooth(along, across, field, first):
    nlat = field.shape[-1]
    for _ in range(STEPS):
        count = field.shape[0]
        flux_lon = along[pl.ds(first, count - 1)] * (field[1:] - field[:-1])
        middle = field[1:-1]
        flux_lat = across[pl.ds(first + 1, count - 2)] * (pltpu.roll(middle, nlat - 1, 2) - middle)
        field = middle + flux_lon[1:] - flux_lon[:-1] + flux_lat - pltpu.roll(flux_lat, 1, 2)
        first += 1
    return field


def thirds(value):
    parts = []
    for _ in range(3):
        part = value.astype(jnp.bfloat16)
        parts.append(part)
        value = value - part.astype(jnp.float32)
    return parts


def matmul(left, right, contract):
    return lax.dot_general(
        left, right, (contract, ((), ())), preferred_element_type=jnp.float32
    )


def hit_matrix(column, percol):
    cell = lax.broadcasted_iota(jnp.int32, (percol, column.shape[1]), 0).astype(jnp.float32)
    return jnp.where(cell == column, 1.0, 0.0).astype(jnp.bfloat16)


def adjoint(weights, hits, values, block):
    spread = weights[block].astype(jnp.float32) * values
    return sum(matmul(part, hits[block], ((1,), (1,))) for part in thirds(spread))


def forward(weights, hits, field):
    flat = jnp.concatenate([field[x] for x in range(field.shape[0])], axis=1)
    picked = sum(matmul(part, hits[1], ((1,), (0,))) for part in thirds(flat))
    return jnp.sum(weights[1].astype(jnp.float32) * picked, axis=0, keepdims=True)


def spread_out(values, weights, hits, field, width):
    for block in range(3):
        flat = adjoint(weights, hits, values[block], block)
        lanes = flat.shape[1] // width
        for x in range(width):
            field[block * width + x] = flat[:, x * lanes : (x + 1) * lanes]


def total(value, lanes):
    return jnp.full((1, lanes), jnp.sum(value), jnp.float32)


def whole_kernel(
    coeffs, payload,
    control, increment, last_in,
    coeffs_low, coeffs_high, low, mine, high, weights, hits, along, across, alphas, gammas, scale,
    precision, field, rhs, rhs_root, residual, residual_root, norm, cross,
    z_out, z_low, z_high, sums_out, sums_in, last_out,
    pay_send, pay_recv, relay_send, relay_recv, side_send, side_recv, sums_send, sums_recv,
    last_send, last_recv,
):
    devices = payload.shape[0]
    me = lax.axis_index("lon")
    below, above = lax.rem(me + devices - 1, devices), lax.rem(me + 1, devices)
    width, levels, nlat = coeffs.shape[1:]
    depth = weights.shape[1]
    slots = precision.shape[1]
    rows = slots // nlat

    def remote(source, target, sent, received, device):
        return pltpu.make_async_remote_copy(
            src_ref=source,
            dst_ref=target,
            send_sem=sent,
            recv_sem=received,
            device_id={"lon": device},
            device_id_type=pl.DeviceIdType.MESH,
        )

    def for_peers(act):
        def step(offset, carry):
            act(lax.rem(me + offset, devices))
            return carry

        lax.fori_loop(1, devices, step, 0)

    def to_sides(source, to_above, to_below, slot):
        return (
            remote(source, to_above, side_send.at[slot], side_recv.at[slot], above),
            remote(source, to_below, side_send.at[slot + 1], side_recv.at[slot + 1], below),
        )

    def relay(source, slab):
        return (
            remote(source, low.at[slab], relay_send.at[0, slab], relay_recv.at[0, slab], above),
            remote(source, high.at[slab], relay_send.at[1, slab], relay_recv.at[1, slab], below),
        )

    barrier = pltpu.get_barrier_semaphore()
    for_peers(
        lambda peer: pl.semaphore_signal(
            barrier, inc=1, device_id={"lon": peer}, device_id_type=pl.DeviceIdType.MESH
        )
    )
    pl.semaphore_wait(barrier, devices - 1)

    for_peers(
        lambda peer: remote(
            payload.at[peer], mine.at[me], pay_send.at[peer], pay_recv.at[me], peer
        ).start()
    )
    coeff_copies = to_sides(coeffs, coeffs_low, coeffs_high, 0)
    for copy in coeff_copies:
        copy.start()
    mine[me] = payload[me]
    for copy in relay(mine.at[me], me):
        copy.start()

    def arrival(peer):
        return remote(payload.at[peer], mine.at[peer], pay_send.at[peer], pay_recv.at[peer], peer)

    def pass_on(peer):
        arrival(peer).wait_recv()
        for copy in relay(mine.at[peer], peer):
            copy.start()

    for_peers(pass_on)

    def take_coeffs(place, source):
        held = pl.ds(place * width, width)
        along[held] = source[0]
        across[held] = source[1]
        factors, inverse = factor_vertical(source[2])
        scale[held] = inverse
        for step, (alpha, gamma) in enumerate(factors):
            alphas[step, held] = alpha
            gammas[step, held] = gamma

    def take_observations(block, source):
        turned = source[...].reshape(slots, source.shape[2]).astype(jnp.float32).T
        weights[block] = turned[:depth].astype(jnp.bfloat16)
        column = turned[depth + 2 : depth + 3] * 16.0 + turned[depth + 3 : depth + 4]
        hits[block] = hit_matrix(column, width * nlat)
        if block == 1:
            precision[...] = turned[depth : depth + 1]
        return turned[depth : depth + 1] * turned[depth + 1 : depth + 2]

    take_coeffs(1, coeffs)
    start_mine = take_observations(1, mine)
    for copy in coeff_copies:
        copy.wait()
    take_coeffs(0, coeffs_low)
    take_coeffs(2, coeffs_high)
    for copy in relay(mine.at[me], me):
        copy.wait()

    def relayed(peer):
        for copy in relay(mine.at[peer], peer):
            copy.wait()

    for_peers(relayed)
    for_peers(lambda peer: arrival(peer).wait_send())
    start_low = take_observations(0, low)
    start_high = take_observations(2, high)
    spread_out((start_low, start_mine, start_high), weights, hits, field, width)
    norm[...] = jnp.zeros_like(norm)

    def first_stage(index, carry):
        part = pl.ds(pl.multiple_of(index * levels, levels), levels)
        solved = solve_vertical(alphas, gammas, scale, field[:, part, :], 0)
        own = smooth(along, across, solved, 0)
        rhs[:, part, :] = own
        inner = own[STEPS : STEPS + width]
        norm[...] += jnp.sum(inner * inner, axis=0)
        rhs_root[:, part, :] = solve_vertical(
            alphas, gammas, scale, smooth(along, across, own, STEPS), width
        )
        return carry

    lax.fori_loop(0, VARS, first_stage, 0)
    seen = forward(weights, hits, rhs_root)
    weighted = precision[...] * seen
    z_out[...] = weighted
    z_copies = to_sides(z_out, z_low, z_high, 2)
    for copy in z_copies:
        copy.start()
    sums_out[0:1, :] = total(norm[...], nlat)
    sums_out[1:2, :] = total(weighted * seen, nlat)
    sums_out[2:8, :] = jnp.zeros((6, nlat), jnp.float32)

    def sums_to(peer):
        return remote(sums_out, sums_in.at[me], sums_send.at[peer], sums_recv.at[me], peer)

    def sums_from(peer):
        return remote(sums_out, sums_in.at[peer], sums_send.at[peer], sums_recv.at[peer], peer)

    for_peers(lambda peer: sums_to(peer).start())
    sums_in[me] = sums_out[...]
    for row in range(rows):
        last_out[row : row + 1, :] = seen[:, row * nlat : (row + 1) * nlat]
    for copy in z_copies:
        copy.wait()
    spread_out((z_low[...], weighted, z_high[...]), weights, hits, field, width)
    for_peers(lambda peer: sums_from(peer).wait())
    sums = jnp.sum(sums_in[...], axis=0)
    first, fit = sums[0:1], sums[1:2]
    alpha = first / (first + fit)
    norm[...] = jnp.zeros_like(norm)
    cross[...] = jnp.zeros_like(cross)

    def second_stage(index, carry):
        part = pl.ds(pl.multiple_of(index * levels, levels), levels)
        solved = solve_vertical(alphas, gammas, scale, field[:, part, :], 0)
        start = rhs[:, part, :]
        image = start + smooth(along, across, solved, 0)
        left = start - alpha[None] * image
        inner = left[STEPS : STEPS + width]
        residual[:, part, :] = inner
        norm[...] += jnp.sum(inner * inner, axis=0)
        cross[...] += jnp.sum(inner * start[STEPS : STEPS + width], axis=0)
        residual_root[:, part, :] = solve_vertical(
            alphas, gammas, scale, smooth(along, across, left, STEPS), width
        )
        return carry

    lax.fori_loop(0, VARS, second_stage, 0)
    seen_rhs = seen
    seen = forward(weights, hits, residual_root)
    weighted = precision[...] * seen
    for row in range(rows):
        last_out[rows + row : rows + row + 1, :] = seen[:, row * nlat : (row + 1) * nlat]
    base = 2 * rows
    last_out[base : base + 1, :] = total(norm[...], nlat)
    last_out[base + 1 : base + 2, :] = total(cross[...], nlat)
    last_out[base + 2 : base + 3, :] = total(weighted * seen, nlat)
    last_out[base + 3 : base + 4, :] = total(weighted * seen_rhs, nlat)
    last_out[base + 4 : base + 8, :] = jnp.zeros((4, nlat), jnp.float32)

    def last_to(peer):
        return remote(last_out, last_in.at[me], last_send.at[peer], last_recv.at[me], peer)

    def last_from(peer):
        return remote(last_out, last_in.at[peer], last_send.at[peer], last_recv.at[peer], peer)

    for_peers(lambda peer: last_to(peer).start())
    last_in[me] = last_out[...]
    for_peers(lambda peer: last_from(peer).wait())
    sums = jnp.sum(last_in[:, base : base + 8, :], axis=0)
    fresh, mixed, fit_fresh, fit_mixed = sums[0:1], sums[1:2], sums[2:3], sums[3:4]
    beta = fresh / first
    curve = fresh + fit_fresh + 2.0 * beta * (mixed + fit_mixed) + beta * beta * (first + fit)
    on_residual = fresh / curve
    on_rhs = alpha + on_residual * beta

    def combine(index, carry):
        part = pl.ds(pl.multiple_of(index * levels, levels), levels)
        own = rhs[STEPS : STEPS + width, part, :]
        control[:, part, :] = on_rhs[None] * own + on_residual[None] * residual[:, part, :]
        increment[:, part, :] = (
            on_rhs[None] * rhs_root[:, part, :] + on_residual[None] * residual_root[:, part, :]
        )
        return carry

    lax.fori_loop(0, VARS, combine, 0)
    last_in[me, base + 4 : base + 5, :] = on_rhs
    last_in[me, base + 5 : base + 6, :] = on_residual


def on_device(
    obs_departure,
    obs_precision,
    obs_columns,
    obs_counts,
    obs_blocks,
    weight_table,
    lon_coeff,
    lat_coeff,
    vert_coeff,
):
    devices = lax.axis_size("lon")
    me = lax.axis_index("lon")
    levels, width, nlat = lon_coeff.shape
    percol = width * nlat
    depth = VARS * LEV
    per_dev = obs_columns.shape[0]
    capacity = max(per_dev // 64, 2 * ((per_dev + devices - 1) // devices), 16)
    slots_all = devices * capacity
    bf16, f32 = jnp.bfloat16, jnp.float32

    open_face = jnp.arange(nlat) < nlat - 1
    coeffs = jnp.stack([lon_coeff, jnp.where(open_face, lat_coeff, 0.0), vert_coeff])
    coeffs = coeffs.transpose(0, 2, 1, 3)

    slot = jnp.arange(per_dev, dtype=jnp.int32)
    live = slot < obs_counts[0]
    owner = obs_columns // percol
    local_col = obs_columns - owner * percol
    hits = (owner[:, None] == jnp.arange(devices, dtype=jnp.int32)) & live[:, None]
    before = jnp.dot(
        (slot[:, None] > slot).astype(bf16), hits.astype(bf16), preferred_element_type=f32
    )
    rank = jnp.sum(jnp.where(hits, before, 0.0), axis=1).astype(jnp.int32)
    target = jnp.where(live, owner * capacity + rank, slots_all)
    place = jnp.arange(slots_all, dtype=jnp.int32)[:, None] == target
    rows = weight_table.shape[0]
    pick = (obs_blocks[:, None] == jnp.arange(rows, dtype=jnp.int32)).astype(bf16)
    block_rows = jnp.dot(pick, weight_table, preferred_element_type=f32).astype(bf16)
    extra = jnp.stack(
        [
            obs_precision,
            obs_departure,
            (local_col // 16).astype(bf16),
            (local_col % 16).astype(bf16),
        ],
        axis=1,
    )
    lanes = -(-(depth + 4) // 128) * 128
    payload = jnp.concatenate([block_rows, extra], axis=1)
    payload = jnp.pad(payload, ((0, 0), (0, lanes - depth - 4)))
    payload = jnp.dot(place.astype(bf16), payload, preferred_element_type=f32).astype(bf16)
    payload = payload.reshape(devices, capacity, lanes)
    wide = 3 * width
    steps = (levels - 1).bit_length()
    rows = slots_all // nlat
    vmem = pl.BlockSpec(memory_space=pltpu.VMEM)
    own_shape = jax.ShapeDtypeStruct((width, depth, nlat), f32)
    last_shape = (2 * rows + 8, nlat)

    def held(*dims, dtype=f32):
        return pltpu.VMEM(dims, dtype)

    dma = pltpu.SemaphoreType.DMA
    control, increment, last = pl.pallas_call(
        whole_kernel,
        out_shape=[own_shape, own_shape, jax.ShapeDtypeStruct((devices,) + last_shape, f32)],
        in_specs=[vmem] * 2,
        out_specs=[vmem] * 3,
        scratch_shapes=[
            held(3, width, levels, nlat),
            held(3, width, levels, nlat),
            held(devices, capacity, lanes, dtype=bf16),
            held(devices, capacity, lanes, dtype=bf16),
            held(devices, capacity, lanes, dtype=bf16),
            held(3, depth, slots_all, dtype=bf16),
            held(3, percol, slots_all, dtype=bf16),
            held(wide, levels, nlat),
            held(wide, levels, nlat),
            held(steps, wide, levels, nlat),
            held(steps, wide, levels, nlat),
            held(wide, levels, nlat),
            held(1, slots_all),
            held(wide, depth, nlat),
            held(width + 2 * STEPS, depth, nlat),
            held(width, depth, nlat),
            held(width, depth, nlat),
            held(width, depth, nlat),
            held(levels, nlat),
            held(levels, nlat),
            held(1, slots_all),
            held(1, slots_all),
            held(1, slots_all),
            held(8, nlat),
            held(devices, 8, nlat),
            held(*last_shape),
            dma((devices,)),
            dma((devices,)),
            dma((2, devices)),
            dma((2, devices)),
            dma((4,)),
            dma((4,)),
            dma((devices,)),
            dma((devices,)),
            dma((devices,)),
            dma((devices,)),
        ],
        compiler_params=pltpu.CompilerParams(
            collective_id=0, has_side_effects=True, vmem_limit_bytes=48 * 2**20
        ),
    )(coeffs, payload)
    on_rhs, on_residual = lax.dynamic_index_in_dim(last, me, 0, False)[2 * rows + 4 : 2 * rows + 6, 0]
    fits = on_rhs * last[:, :rows] + on_residual * last[:, rows : 2 * rows]
    fits = fits.reshape(devices, slots_all)
    fit = lax.dynamic_slice_in_dim(fits, me * capacity, capacity, axis=1)
    fit = jnp.dot(fit.reshape(1, slots_all), place.astype(f32), precision=EXACT)[0]
    obs_fit = jnp.where(live, fit - obs_departure.astype(f32), 0.0)

    def placed(field):
        return field.reshape(width, VARS, levels, nlat).transpose(1, 2, 0, 3)

    return placed(control), placed(increment), obs_fit


def solution(mesh):
    in_specs = (
        P(("member", "lon")),
        P("lon"),
        P("lon"),
        P("lon"),
        P("lon"),
        P("lon", None),
        P(None, "lon", None),
        P(None, "lon", None),
        P(None, "lon", None),
    )
    out_specs = (
        P("member", None, "lon", None),
        P("member", None, "lon", None),
        P(("member", "lon")),
    )
    return jax.shard_map(
        on_device, mesh=mesh, in_specs=in_specs, out_specs=out_specs, check_vma=False
    )
```

```python
import jax
import jax.numpy as jnp
from jax import lax
from jax.experimental import pallas as pl
from jax.experimental.pallas import tpu as pltpu
from jax.sharding import PartitionSpec as P

VARS = 6
LEV = 32
STEPS = 2


def factor_vertical(vert):
    levels = vert.shape[-2]
    level = lax.broadcasted_iota(jnp.int32, vert.shape, vert.ndim - 2)
    axis = vert.ndim - 2
    upward = jnp.where(level < levels - 1, vert, 0.0)
    downward = jnp.where(level > 0, pltpu.roll(upward, 1, axis), 0.0)
    lower, upper = -downward, -upward
    diag = 1.0 + downward + upward
    factors = []
    stride = 1
    while stride < levels:
        back = levels - stride
        alpha = -lower / pltpu.roll(diag, stride, axis)
        gamma = -upper / pltpu.roll(diag, back, axis)
        new_lower = alpha * pltpu.roll(lower, stride, axis)
        new_upper = gamma * pltpu.roll(upper, back, axis)
        diag = diag + alpha * pltpu.roll(upper, stride, axis) + gamma * pltpu.roll(lower, back, axis)
        factors.append((alpha, gamma))
        lower, upper = new_lower, new_upper
        stride *= 2
    return factors, 1.0 / diag


def solve_vertical(alphas, gammas, scale, field, first):
    count, levels = field.shape[:2]
    held = pl.ds(first, count)
    for step in range(alphas.shape[0]):
        stride = 2**step
        field = (
            field
            + alphas[step, held] * pltpu.roll(field, stride, 1)
            + gammas[step, held] * pltpu.roll(field, levels - stride, 1)
        )
    return field * scale[held]


def smooth(along, across, field, first):
    nlat = field.shape[-1]
    for _ in range(STEPS):
        count = field.shape[0]
        flux_lon = along[pl.ds(first, count - 1)] * (field[1:] - field[:-1])
        middle = field[1:-1]
        flux_lat = across[pl.ds(first + 1, count - 2)] * (pltpu.roll(middle, nlat - 1, 2) - middle)
        field = middle + flux_lon[1:] - flux_lon[:-1] + flux_lat - pltpu.roll(flux_lat, 1, 2)
        first += 1
    return field


def thirds(value):
    parts = []
    for _ in range(3):
        part = value.astype(jnp.bfloat16)
        parts.append(part)
        value = value - part.astype(jnp.float32)
    return parts


def matmul(left, right, contract):
    return lax.dot_general(
        left, right, (contract, ((), ())), preferred_element_type=jnp.float32
    )


def hit_matrix(column, percol):
    cell = lax.broadcasted_iota(jnp.int32, (percol, column.shape[1]), 0).astype(jnp.float32)
    return jnp.where(cell == column, 1.0, 0.0).astype(jnp.bfloat16)


def adjoint(weights, hits, values, block):
    spread = weights[block].astype(jnp.float32) * values
    return sum(matmul(part, hits[block], ((1,), (1,))) for part in thirds(spread))


def forward(weights, hits, field):
    flat = jnp.concatenate([field[x] for x in range(field.shape[0])], axis=1)
    picked = sum(matmul(part, hits[1], ((1,), (0,))) for part in thirds(flat))
    return jnp.sum(weights[1].astype(jnp.float32) * picked, axis=0, keepdims=True)


def spread_out(values, weights, hits, field, width):
    for block in range(3):
        flat = adjoint(weights, hits, values[block], block)
        lanes = flat.shape[1] // width
        for x in range(width):
            field[block * width + x] = flat[:, x * lanes : (x + 1) * lanes]


def total(value, lanes):
    return jnp.full((1, lanes), jnp.sum(value), jnp.float32)


def whole_kernel(
    departures, precisions, columns, counts, blocks, table, lon, lat, vert,
    control, increment, obs_fit,
    coeffs, payload, last_in, wide_table, extras, coeffs_low, coeffs_high, low, mine, high, weights, hits, along, across, alphas, gammas, scale,
    precision, field, rhs, rhs_root, residual, residual_root, norm, cross,
    z_out, z_low, z_high, sums_out, sums_in, last_out,
    pay_send, pay_recv, relay_send, relay_recv, side_send, side_recv, sums_send, sums_recv,
    last_send, last_recv,
):
    devices, capacity, lanes = payload.shape
    me = lax.axis_index("lon")
    below, above = lax.rem(me + devices - 1, devices), lax.rem(me + 1, devices)
    width, levels, nlat = coeffs.shape[1:]
    depth = weights.shape[1]
    slots = precision.shape[1]
    rows = slots // nlat

    def remote(source, target, sent, received, device):
        return pltpu.make_async_remote_copy(
            src_ref=source,
            dst_ref=target,
            send_sem=sent,
            recv_sem=received,
            device_id={"lon": device},
            device_id_type=pl.DeviceIdType.MESH,
        )

    def for_peers(act):
        def step(offset, carry):
            act(lax.rem(me + offset, devices))
            return carry

        lax.fori_loop(1, devices, step, 0)

    def to_sides(source, to_above, to_below, slot):
        return (
            remote(source, to_above, side_send.at[slot], side_recv.at[slot], above),
            remote(source, to_below, side_send.at[slot + 1], side_recv.at[slot + 1], below),
        )

    def relay(source, slab):
        return (
            remote(source, low.at[slab], relay_send.at[0, slab], relay_recv.at[0, slab], above),
            remote(source, high.at[slab], relay_send.at[1, slab], relay_recv.at[1, slab], below),
        )

    barrier = pltpu.get_barrier_semaphore()
    for_peers(
        lambda peer: pl.semaphore_signal(
            barrier, inc=1, device_id={"lon": peer}, device_id_type=pl.DeviceIdType.MESH
        )
    )
    for x in range(width):
        coeffs[0, x] = lon[:, x, :]
        across_own = lat[:, x, :]
        face = lax.broadcasted_iota(jnp.int32, across_own.shape, 1)
        coeffs[1, x] = jnp.where(face < nlat - 1, across_own, 0.0)
        coeffs[2, x] = vert[:, x, :]
    pl.semaphore_wait(barrier, devices - 1)
    coeff_copies = to_sides(coeffs, coeffs_low, coeffs_high, 0)
    for copy in coeff_copies:
        copy.start()

    per_dev = columns.shape[1]
    percol = float(width * nlat)
    bf16, f32 = jnp.bfloat16, jnp.float32
    live = lax.broadcasted_iota(jnp.int32, (1, per_dev), 1) < counts[0, 0]
    column = columns[...].astype(f32)
    owner = jnp.floor((column + 0.5) * (1.0 / percol))
    local = column - owner * percol
    local_high = jnp.floor((local + 0.5) * (1.0 / 16.0))
    device_row = lax.broadcasted_iota(jnp.int32, (devices, per_dev), 0).astype(f32)
    owned = jnp.where((device_row == owner) & live, 1.0, 0.0)
    earlier = (
        lax.broadcasted_iota(jnp.int32, (per_dev, per_dev), 0)
        < lax.broadcasted_iota(jnp.int32, (per_dev, per_dev), 1)
    )
    earlier = jnp.where(earlier, 1.0, 0.0).astype(bf16)
    before = matmul(owned.astype(bf16), earlier, ((1,), (0,)))
    rank = jnp.sum(owned * before, axis=0, keepdims=True)
    target = jnp.where(live, owner * float(capacity) + rank, float(slots))
    slot_row = lax.broadcasted_iota(jnp.int32, (slots, per_dev), 0).astype(f32)
    place = jnp.where(slot_row == target, 1.0, 0.0).astype(bf16)
    table_row = lax.broadcasted_iota(jnp.int32, (table.shape[0], per_dev), 0)
    pick = jnp.where(table_row == blocks[...], 1.0, 0.0).astype(bf16)
    slot_pick = matmul(place, pick, ((1,), (1,))).astype(bf16)
    wide_table[...] = jnp.zeros_like(wide_table)
    wide_table[:, 0:depth] = table[...]
    extras[...] = jnp.zeros_like(extras)
    extras[depth : depth + 1, :] = precisions[...]
    extras[depth + 1 : depth + 2, :] = departures[...]
    extras[depth + 2 : depth + 3, :] = local_high
    extras[depth + 3 : depth + 4, :] = local - local_high * 16.0
    filled = matmul(slot_pick, wide_table[...], ((1,), (0,)))
    filled += matmul(place, extras[...].astype(bf16), ((1,), (1,)))
    payload[...] = filled.astype(bf16).reshape(devices, capacity, lanes)


    for_peers(
        lambda peer: remote(
            payload.at[peer], mine.at[me], pay_send.at[peer], pay_recv.at[me], peer
        ).start()
    )
    mine[me] = payload[me]
    for copy in relay(mine.at[me], me):
        copy.start()

    def arrival(peer):
        return remote(payload.at[peer], mine.at[peer], pay_send.at[peer], pay_recv.at[peer], peer)

    def pass_on(peer):
        arrival(peer).wait_recv()
        for copy in relay(mine.at[peer], peer):
            copy.start()

    for_peers(pass_on)

    def take_coeffs(place, source):
        held = pl.ds(place * width, width)
        along[held] = source[0]
        across[held] = source[1]
        factors, inverse = factor_vertical(source[2])
        scale[held] = inverse
        for step, (alpha, gamma) in enumerate(factors):
            alphas[step, held] = alpha
            gammas[step, held] = gamma

    def take_observations(block, source):
        turned = source[...].reshape(slots, source.shape[2]).astype(jnp.float32).T
        weights[block] = turned[:depth].astype(jnp.bfloat16)
        column = turned[depth + 2 : depth + 3] * 16.0 + turned[depth + 3 : depth + 4]
        hits[block] = hit_matrix(column, width * nlat)
        if block == 1:
            precision[...] = turned[depth : depth + 1]
        return turned[depth : depth + 1] * turned[depth + 1 : depth + 2]

    take_coeffs(1, coeffs)
    start_mine = take_observations(1, mine)
    for copy in coeff_copies:
        copy.wait()
    take_coeffs(0, coeffs_low)
    take_coeffs(2, coeffs_high)
    for copy in relay(mine.at[me], me):
        copy.wait()

    def relayed(peer):
        for copy in relay(mine.at[peer], peer):
            copy.wait()

    for_peers(relayed)
    for_peers(lambda peer: arrival(peer).wait_send())
    start_low = take_observations(0, low)
    start_high = take_observations(2, high)
    spread_out((start_low, start_mine, start_high), weights, hits, field, width)
    norm[...] = jnp.zeros_like(norm)

    def first_stage(index, carry):
        part = pl.ds(pl.multiple_of(index * levels, levels), levels)
        solved = solve_vertical(alphas, gammas, scale, field[:, part, :], 0)
        own = smooth(along, across, solved, 0)
        rhs[:, part, :] = own
        inner = own[STEPS : STEPS + width]
        norm[...] += jnp.sum(inner * inner, axis=0)
        rhs_root[:, part, :] = solve_vertical(
            alphas, gammas, scale, smooth(along, across, own, STEPS), width
        )
        return carry

    lax.fori_loop(0, VARS, first_stage, 0)
    seen = forward(weights, hits, rhs_root)
    weighted = precision[...] * seen
    z_out[...] = weighted
    z_copies = to_sides(z_out, z_low, z_high, 2)
    for copy in z_copies:
        copy.start()
    sums_out[0:1, :] = total(norm[...], nlat)
    sums_out[1:2, :] = total(weighted * seen, nlat)
    sums_out[2:8, :] = jnp.zeros((6, nlat), jnp.float32)

    def sums_to(peer):
        return remote(sums_out, sums_in.at[me], sums_send.at[peer], sums_recv.at[me], peer)

    def sums_from(peer):
        return remote(sums_out, sums_in.at[peer], sums_send.at[peer], sums_recv.at[peer], peer)

    for_peers(lambda peer: sums_to(peer).start())
    sums_in[me] = sums_out[...]
    for row in range(rows):
        last_out[row : row + 1, :] = seen[:, row * nlat : (row + 1) * nlat]
    for copy in z_copies:
        copy.wait()
    spread_out((z_low[...], weighted, z_high[...]), weights, hits, field, width)
    for_peers(lambda peer: sums_from(peer).wait())
    sums = jnp.sum(sums_in[...], axis=0)
    first, fit = sums[0:1], sums[1:2]
    alpha = first / (first + fit)
    norm[...] = jnp.zeros_like(norm)
    cross[...] = jnp.zeros_like(cross)

    def second_stage(index, carry):
        part = pl.ds(pl.multiple_of(index * levels, levels), levels)
        solved = solve_vertical(alphas, gammas, scale, field[:, part, :], 0)
        start = rhs[:, part, :]
        image = start + smooth(along, across, solved, 0)
        left = start - alpha[None] * image
        inner = left[STEPS : STEPS + width]
        residual[:, part, :] = inner
        norm[...] += jnp.sum(inner * inner, axis=0)
        cross[...] += jnp.sum(inner * start[STEPS : STEPS + width], axis=0)
        residual_root[:, part, :] = solve_vertical(
            alphas, gammas, scale, smooth(along, across, left, STEPS), width
        )
        return carry

    lax.fori_loop(0, VARS, second_stage, 0)
    seen_rhs = seen
    seen = forward(weights, hits, residual_root)
    weighted = precision[...] * seen
    for row in range(rows):
        last_out[rows + row : rows + row + 1, :] = seen[:, row * nlat : (row + 1) * nlat]
    base = 2 * rows
    last_out[base : base + 1, :] = total(norm[...], nlat)
    last_out[base + 1 : base + 2, :] = total(cross[...], nlat)
    last_out[base + 2 : base + 3, :] = total(weighted * seen, nlat)
    last_out[base + 3 : base + 4, :] = total(weighted * seen_rhs, nlat)
    last_out[base + 4 : base + 8, :] = jnp.zeros((4, nlat), jnp.float32)

    def last_to(peer):
        return remote(last_out, last_in.at[me], last_send.at[peer], last_recv.at[me], peer)

    def last_from(peer):
        return remote(last_out, last_in.at[peer], last_send.at[peer], last_recv.at[peer], peer)

    for_peers(lambda peer: last_to(peer).start())
    last_in[me] = last_out[...]
    for_peers(lambda peer: last_from(peer).wait())
    sums = jnp.sum(last_in[:, base : base + 8, :], axis=0)
    fresh, mixed, fit_fresh, fit_mixed = sums[0:1], sums[1:2], sums[2:3], sums[3:4]
    beta = fresh / first
    curve = fresh + fit_fresh + 2.0 * beta * (mixed + fit_mixed) + beta * beta * (first + fit)
    on_residual = fresh / curve
    on_rhs = alpha + on_residual * beta

    def combine(index, carry):
        part = pl.ds(pl.multiple_of(index * levels, levels), levels)
        own = rhs[STEPS : STEPS + width, part, :]
        control[:, part, :] = on_rhs[None] * own + on_residual[None] * residual[:, part, :]
        increment[:, part, :] = (
            on_rhs[None] * rhs_root[:, part, :] + on_residual[None] * residual_root[:, part, :]
        )
        return carry

    lax.fori_loop(0, VARS, combine, 0)
    begin = me * capacity
    row = begin // nlat
    lane = (begin - row * nlat).astype(f32) + rank
    fits = on_rhs * last_in[:, row, :] + on_residual * last_in[:, rows + row, :]
    lane_row = lax.broadcasted_iota(jnp.int32, (nlat, per_dev), 0).astype(f32)
    at_lane = jnp.where(lane_row == lane, 1.0, 0.0).astype(bf16)
    spread = sum(matmul(part, at_lane, ((1,), (0,))) for part in thirds(fits))
    fit = jnp.sum(owned * spread, axis=0, keepdims=True)
    obs_fit[...] = jnp.where(live, fit - departures[...], 0.0)


def on_device(
    obs_departure,
    obs_precision,
    obs_columns,
    obs_counts,
    obs_blocks,
    weight_table,
    lon_coeff,
    lat_coeff,
    vert_coeff,
):
    devices = lax.axis_size("lon")
    levels, width, nlat = lon_coeff.shape
    percol = width * nlat
    depth = VARS * LEV
    per_dev = obs_columns.shape[0]
    capacity = max(per_dev // 64, 2 * ((per_dev + devices - 1) // devices), 16)
    slots_all = devices * capacity
    bf16, f32 = jnp.bfloat16, jnp.float32

    lanes = -(-(depth + 4) // 128) * 128
    wide = 3 * width
    steps = (levels - 1).bit_length()
    rows = slots_all // nlat
    vmem = pl.BlockSpec(memory_space=pltpu.VMEM)
    own_shape = jax.ShapeDtypeStruct((width, depth, nlat), f32)
    last_shape = (2 * rows + 8, nlat)

    def held(*dims, dtype=f32):
        return pltpu.VMEM(dims, dtype)

    dma = pltpu.SemaphoreType.DMA
    control, increment, obs_fit = pl.pallas_call(
        whole_kernel,
        out_shape=[own_shape, own_shape, jax.ShapeDtypeStruct((1, per_dev), f32)],
        in_specs=[vmem] * 3 + [pl.BlockSpec(memory_space=pltpu.SMEM)] + [vmem] * 5,
        out_specs=[vmem] * 3,
        scratch_shapes=[
            held(3, width, levels, nlat),
            held(devices, capacity, lanes, dtype=bf16),
            held(devices, *last_shape),
            held(weight_table.shape[0], lanes, dtype=bf16),
            held(lanes, per_dev),
            held(3, width, levels, nlat),
            held(3, width, levels, nlat),
            held(devices, capacity, lanes, dtype=bf16),
            held(devices, capacity, lanes, dtype=bf16),
            held(devices, capacity, lanes, dtype=bf16),
            held(3, depth, slots_all, dtype=bf16),
            held(3, percol, slots_all, dtype=bf16),
            held(wide, levels, nlat),
            held(wide, levels, nlat),
            held(steps, wide, levels, nlat),
            held(steps, wide, levels, nlat),
            held(wide, levels, nlat),
            held(1, slots_all),
            held(wide, depth, nlat),
            held(width + 2 * STEPS, depth, nlat),
            held(width, depth, nlat),
            held(width, depth, nlat),
            held(width, depth, nlat),
            held(levels, nlat),
            held(levels, nlat),
            held(1, slots_all),
            held(1, slots_all),
            held(1, slots_all),
            held(8, nlat),
            held(devices, 8, nlat),
            held(*last_shape),
            dma((devices,)),
            dma((devices,)),
            dma((2, devices)),
            dma((2, devices)),
            dma((4,)),
            dma((4,)),
            dma((devices,)),
            dma((devices,)),
            dma((devices,)),
            dma((devices,)),
        ],
        compiler_params=pltpu.CompilerParams(
            collective_id=0, has_side_effects=True, vmem_limit_bytes=48 * 2**20
        ),
    )(
        obs_departure.astype(f32).reshape(1, per_dev),
        obs_precision.astype(f32).reshape(1, per_dev),
        obs_columns.reshape(1, per_dev),
        obs_counts.reshape(1, 1),
        obs_blocks.reshape(1, per_dev),
        weight_table,
        lon_coeff,
        lat_coeff,
        vert_coeff,
    )

    def placed(field):
        return field.reshape(width, VARS, levels, nlat).transpose(1, 2, 0, 3)

    return placed(control), placed(increment), obs_fit.reshape(per_dev)


def solution(mesh):
    in_specs = (
        P(("member", "lon")),
        P("lon"),
        P("lon"),
        P("lon"),
        P("lon"),
        P("lon", None),
        P(None, "lon", None),
        P(None, "lon", None),
        P(None, "lon", None),
    )
    out_specs = (
        P("member", None, "lon", None),
        P("member", None, "lon", None),
        P(("member", "lon")),
    )
    return jax.shard_map(
        on_device, mesh=mesh, in_specs=in_specs, out_specs=out_specs, check_vma=False
    )
```

```python
import jax
import jax.numpy as jnp
from jax import lax
from jax.experimental import pallas as pl
from jax.experimental.pallas import tpu as pltpu
from jax.sharding import PartitionSpec as P

VARS = 6
LEV = 32
STEPS = 2


def factor_vertical(vert):
    levels = vert.shape[-2]
    level = lax.broadcasted_iota(jnp.int32, vert.shape, vert.ndim - 2)
    axis = vert.ndim - 2
    upward = jnp.where(level < levels - 1, vert, 0.0)
    downward = jnp.where(level > 0, pltpu.roll(upward, 1, axis), 0.0)
    lower, upper = -downward, -upward
    diag = 1.0 + downward + upward
    factors = []
    stride = 1
    while stride < levels:
        back = levels - stride
        alpha = -lower / pltpu.roll(diag, stride, axis)
        gamma = -upper / pltpu.roll(diag, back, axis)
        new_lower = alpha * pltpu.roll(lower, stride, axis)
        new_upper = gamma * pltpu.roll(upper, back, axis)
        diag = diag + alpha * pltpu.roll(upper, stride, axis) + gamma * pltpu.roll(lower, back, axis)
        factors.append((alpha, gamma))
        lower, upper = new_lower, new_upper
        stride *= 2
    return factors, 1.0 / diag


def solve_vertical(alphas, gammas, scale, field, first):
    count, levels = field.shape[:2]
    held = pl.ds(first, count)
    for step in range(alphas.shape[0]):
        stride = 2**step
        field = (
            field
            + alphas[step, held] * pltpu.roll(field, stride, 1)
            + gammas[step, held] * pltpu.roll(field, levels - stride, 1)
        )
    return field * scale[held]


def smooth(along, across, field, first):
    nlat = field.shape[-1]
    for _ in range(STEPS):
        count = field.shape[0]
        flux_lon = along[pl.ds(first, count - 1)] * (field[1:] - field[:-1])
        middle = field[1:-1]
        flux_lat = across[pl.ds(first + 1, count - 2)] * (pltpu.roll(middle, nlat - 1, 2) - middle)
        field = middle + flux_lon[1:] - flux_lon[:-1] + flux_lat - pltpu.roll(flux_lat, 1, 2)
        first += 1
    return field


def thirds(value):
    parts = []
    for _ in range(3):
        part = value.astype(jnp.bfloat16)
        parts.append(part)
        value = value - part.astype(jnp.float32)
    return parts


def matmul(left, right, contract):
    return lax.dot_general(
        left, right, (contract, ((), ())), preferred_element_type=jnp.float32
    )


def hit_matrix(column, percol):
    cell = lax.broadcasted_iota(jnp.int32, (percol, column.shape[1]), 0).astype(jnp.float32)
    return jnp.where(cell == column, 1.0, 0.0).astype(jnp.bfloat16)


def adjoint(weights, hits, values, block):
    spread = weights[block].astype(jnp.float32) * values
    return sum(matmul(part, hits[block], ((1,), (1,))) for part in thirds(spread))


def forward(weights, hits, field):
    flat = jnp.concatenate([field[x] for x in range(field.shape[0])], axis=1)
    picked = sum(matmul(part, hits[1], ((1,), (0,))) for part in thirds(flat))
    return jnp.sum(weights[1].astype(jnp.float32) * picked, axis=0, keepdims=True)


def spread_out(values, weights, hits, field, width):
    for block in range(3):
        flat = adjoint(weights, hits, values[block], block)
        lanes = flat.shape[1] // width
        for x in range(width):
            field[block * width + x] = flat[:, x * lanes : (x + 1) * lanes]


def total(value, lanes):
    return jnp.full((1, lanes), jnp.sum(value), jnp.float32)


def whole_kernel(
    loads,
    departures, precisions, columns, counts, blocks, table, lon, lat, vert,
    control, increment, obs_fit,
    coeffs, payload, last_in, wide_table, extras, coeffs_low, coeffs_high, low, mine, high, weights, hits, along, across, alphas, gammas, scale,
    precision, field, rhs, rhs_root, residual, residual_root, norm, cross,
    z_out, z_low, z_high, sums_out, sums_in, last_out,
    pay_send, pay_recv, relay_send, relay_recv, side_send, side_recv, sums_send, sums_recv,
    last_send, last_recv,
):
    devices, capacity, lanes = payload.shape
    me = lax.axis_index("lon")
    below, above = lax.rem(me + devices - 1, devices), lax.rem(me + 1, devices)
    width, levels, nlat = coeffs.shape[1:]
    depth = weights.shape[1]
    slots = precision.shape[1]
    rows = slots // nlat

    def remote(source, target, sent, received, device):
        return pltpu.make_async_remote_copy(
            src_ref=source,
            dst_ref=target,
            send_sem=sent,
            recv_sem=received,
            device_id={"lon": device},
            device_id_type=pl.DeviceIdType.MESH,
        )

    def for_peers(act):
        def step(offset, carry):
            act(lax.rem(me + offset, devices))
            return carry

        lax.fori_loop(1, devices, step, 0)

    def to_sides(source, to_above, to_below, slot):
        return (
            remote(source, to_above, side_send.at[slot], side_recv.at[slot], above),
            remote(source, to_below, side_send.at[slot + 1], side_recv.at[slot + 1], below),
        )

    def relay(source, slab):
        return (
            remote(source, low.at[slab], relay_send.at[0, slab], relay_recv.at[0, slab], above),
            remote(source, high.at[slab], relay_send.at[1, slab], relay_recv.at[1, slab], below),
        )

    barrier = pltpu.get_barrier_semaphore()
    for_peers(
        lambda peer: pl.semaphore_signal(
            barrier, inc=1, device_id={"lon": peer}, device_id_type=pl.DeviceIdType.MESH
        )
    )
    for copy in loads:
        copy.wait()
    for x in range(width):
        coeffs[0, x] = lon[:, x, :]
        across_own = lat[:, x, :]
        face = lax.broadcasted_iota(jnp.int32, across_own.shape, 1)
        coeffs[1, x] = jnp.where(face < nlat - 1, across_own, 0.0)
        coeffs[2, x] = vert[:, x, :]
    pl.semaphore_wait(barrier, devices - 1)
    coeff_copies = to_sides(coeffs, coeffs_low, coeffs_high, 0)
    for copy in coeff_copies:
        copy.start()

    per_dev = columns.shape[1]
    percol = float(width * nlat)
    bf16, f32 = jnp.bfloat16, jnp.float32
    live = lax.broadcasted_iota(jnp.int32, (1, per_dev), 1) < counts[0, 0]
    column = columns[...].astype(f32)
    owner = jnp.floor((column + 0.5) * (1.0 / percol))
    local = column - owner * percol
    local_high = jnp.floor((local + 0.5) * (1.0 / 16.0))
    device_row = lax.broadcasted_iota(jnp.int32, (devices, per_dev), 0).astype(f32)
    owned = jnp.where((device_row == owner) & live, 1.0, 0.0)
    earlier = (
        lax.broadcasted_iota(jnp.int32, (per_dev, per_dev), 0)
        < lax.broadcasted_iota(jnp.int32, (per_dev, per_dev), 1)
    )
    earlier = jnp.where(earlier, 1.0, 0.0).astype(bf16)
    before = matmul(owned.astype(bf16), earlier, ((1,), (0,)))
    rank = jnp.sum(owned * before, axis=0, keepdims=True)
    target = jnp.where(live, owner * float(capacity) + rank, float(slots))
    slot_row = lax.broadcasted_iota(jnp.int32, (slots, per_dev), 0).astype(f32)
    place = jnp.where(slot_row == target, 1.0, 0.0).astype(bf16)
    table_row = lax.broadcasted_iota(jnp.int32, (table.shape[0], per_dev), 0)
    pick = jnp.where(table_row == blocks[...], 1.0, 0.0).astype(bf16)
    slot_pick = matmul(place, pick, ((1,), (1,))).astype(bf16)
    wide_table[...] = jnp.zeros_like(wide_table)
    wide_table[:, 0:depth] = table[...]
    extras[...] = jnp.zeros_like(extras)
    extras[depth : depth + 1, :] = precisions[...]
    extras[depth + 1 : depth + 2, :] = departures[...]
    extras[depth + 2 : depth + 3, :] = local_high
    extras[depth + 3 : depth + 4, :] = local - local_high * 16.0
    filled = matmul(slot_pick, wide_table[...], ((1,), (0,)))
    filled += matmul(place, extras[...].astype(bf16), ((1,), (1,)))
    payload[...] = filled.astype(bf16).reshape(devices, capacity, lanes)


    for_peers(
        lambda peer: remote(
            payload.at[peer], mine.at[me], pay_send.at[peer], pay_recv.at[me], peer
        ).start()
    )
    mine[me] = payload[me]
    for copy in relay(mine.at[me], me):
        copy.start()

    def arrival(peer):
        return remote(payload.at[peer], mine.at[peer], pay_send.at[peer], pay_recv.at[peer], peer)

    def pass_on(peer):
        arrival(peer).wait_recv()
        for copy in relay(mine.at[peer], peer):
            copy.start()

    for_peers(pass_on)

    def take_coeffs(place, source):
        held = pl.ds(place * width, width)
        along[held] = source[0]
        across[held] = source[1]
        factors, inverse = factor_vertical(source[2])
        scale[held] = inverse
        for step, (alpha, gamma) in enumerate(factors):
            alphas[step, held] = alpha
            gammas[step, held] = gamma

    def take_observations(block, source):
        turned = source[...].reshape(slots, source.shape[2]).astype(jnp.float32).T
        weights[block] = turned[:depth].astype(jnp.bfloat16)
        column = turned[depth + 2 : depth + 3] * 16.0 + turned[depth + 3 : depth + 4]
        hits[block] = hit_matrix(column, width * nlat)
        if block == 1:
            precision[...] = turned[depth : depth + 1]
        return turned[depth : depth + 1] * turned[depth + 1 : depth + 2]

    take_coeffs(1, coeffs)
    start_mine = take_observations(1, mine)
    for copy in coeff_copies:
        copy.wait()
    take_coeffs(0, coeffs_low)
    take_coeffs(2, coeffs_high)
    for copy in relay(mine.at[me], me):
        copy.wait()

    def relayed(peer):
        for copy in relay(mine.at[peer], peer):
            copy.wait()

    for_peers(relayed)
    for_peers(lambda peer: arrival(peer).wait_send())
    start_low = take_observations(0, low)
    start_high = take_observations(2, high)
    spread_out((start_low, start_mine, start_high), weights, hits, field, width)
    norm[...] = jnp.zeros_like(norm)

    def first_stage(index, carry):
        part = pl.ds(pl.multiple_of(index * levels, levels), levels)
        solved = solve_vertical(alphas, gammas, scale, field[:, part, :], 0)
        own = smooth(along, across, solved, 0)
        rhs[:, part, :] = own
        inner = own[STEPS : STEPS + width]
        norm[...] += jnp.sum(inner * inner, axis=0)
        rhs_root[:, part, :] = solve_vertical(
            alphas, gammas, scale, smooth(along, across, own, STEPS), width
        )
        return carry

    lax.fori_loop(0, VARS, first_stage, 0)
    seen = forward(weights, hits, rhs_root)
    weighted = precision[...] * seen
    z_out[...] = weighted
    z_copies = to_sides(z_out, z_low, z_high, 2)
    for copy in z_copies:
        copy.start()
    sums_out[0:1, :] = total(norm[...], nlat)
    sums_out[1:2, :] = total(weighted * seen, nlat)
    sums_out[2:8, :] = jnp.zeros((6, nlat), jnp.float32)

    def sums_to(peer):
        return remote(sums_out, sums_in.at[me], sums_send.at[peer], sums_recv.at[me], peer)

    def sums_from(peer):
        return remote(sums_out, sums_in.at[peer], sums_send.at[peer], sums_recv.at[peer], peer)

    for_peers(lambda peer: sums_to(peer).start())
    sums_in[me] = sums_out[...]
    for row in range(rows):
        last_out[row : row + 1, :] = seen[:, row * nlat : (row + 1) * nlat]
    for copy in z_copies:
        copy.wait()
    spread_out((z_low[...], weighted, z_high[...]), weights, hits, field, width)
    for_peers(lambda peer: sums_from(peer).wait())
    sums = jnp.sum(sums_in[...], axis=0)
    first, fit = sums[0:1], sums[1:2]
    alpha = first / (first + fit)
    norm[...] = jnp.zeros_like(norm)
    cross[...] = jnp.zeros_like(cross)

    def second_stage(index, carry):
        part = pl.ds(pl.multiple_of(index * levels, levels), levels)
        solved = solve_vertical(alphas, gammas, scale, field[:, part, :], 0)
        start = rhs[:, part, :]
        image = start + smooth(along, across, solved, 0)
        left = start - alpha[None] * image
        inner = left[STEPS : STEPS + width]
        residual[:, part, :] = inner
        norm[...] += jnp.sum(inner * inner, axis=0)
        cross[...] += jnp.sum(inner * start[STEPS : STEPS + width], axis=0)
        residual_root[:, part, :] = solve_vertical(
            alphas, gammas, scale, smooth(along, across, left, STEPS), width
        )
        return carry

    lax.fori_loop(0, VARS, second_stage, 0)
    seen_rhs = seen
    seen = forward(weights, hits, residual_root)
    weighted = precision[...] * seen
    for row in range(rows):
        last_out[rows + row : rows + row + 1, :] = seen[:, row * nlat : (row + 1) * nlat]
    base = 2 * rows
    last_out[base : base + 1, :] = total(norm[...], nlat)
    last_out[base + 1 : base + 2, :] = total(cross[...], nlat)
    last_out[base + 2 : base + 3, :] = total(weighted * seen, nlat)
    last_out[base + 3 : base + 4, :] = total(weighted * seen_rhs, nlat)
    last_out[base + 4 : base + 8, :] = jnp.zeros((4, nlat), jnp.float32)

    def last_to(peer):
        return remote(last_out, last_in.at[me], last_send.at[peer], last_recv.at[me], peer)

    def last_from(peer):
        return remote(last_out, last_in.at[peer], last_send.at[peer], last_recv.at[peer], peer)

    for_peers(lambda peer: last_to(peer).start())
    last_in[me] = last_out[...]
    for_peers(lambda peer: last_from(peer).wait())
    sums = jnp.sum(last_in[:, base : base + 8, :], axis=0)
    fresh, mixed, fit_fresh, fit_mixed = sums[0:1], sums[1:2], sums[2:3], sums[3:4]
    beta = fresh / first
    curve = fresh + fit_fresh + 2.0 * beta * (mixed + fit_mixed) + beta * beta * (first + fit)
    on_residual = fresh / curve
    on_rhs = alpha + on_residual * beta

    def combine(index, carry):
        part = pl.ds(pl.multiple_of(index * levels, levels), levels)
        own = rhs[STEPS : STEPS + width, part, :]
        control[:, part, :] = on_rhs[None] * own + on_residual[None] * residual[:, part, :]
        increment[:, part, :] = (
            on_rhs[None] * rhs_root[:, part, :] + on_residual[None] * residual_root[:, part, :]
        )
        return carry

    lax.fori_loop(0, VARS, combine, 0)
    begin = me * capacity
    row = begin // nlat
    lane = (begin - row * nlat).astype(f32) + rank
    fits = on_rhs * last_in[:, row, :] + on_residual * last_in[:, rows + row, :]
    lane_row = lax.broadcasted_iota(jnp.int32, (nlat, per_dev), 0).astype(f32)
    at_lane = jnp.where(lane_row == lane, 1.0, 0.0).astype(bf16)
    spread = sum(matmul(part, at_lane, ((1,), (0,))) for part in thirds(fits))
    fit = jnp.sum(owned * spread, axis=0, keepdims=True)
    obs_fit[...] = jnp.where(live, fit - departures[...], 0.0)


def loading_kernel(*refs):
    sources, rest = refs[:9], refs[9:-9]
    targets, sems = refs[-9:-1], refs[-1]
    targets = targets[:3] + (sources[3],) + targets[3:]
    loads = [
        pltpu.make_async_copy(sources[i], targets[i], sems.at[i]) for i in range(9) if i != 3
    ]
    for copy in loads:
        copy.start()
    whole_kernel(loads, *targets, *rest)


def on_device(
    obs_departure,
    obs_precision,
    obs_columns,
    obs_counts,
    obs_blocks,
    weight_table,
    lon_coeff,
    lat_coeff,
    vert_coeff,
):
    devices = lax.axis_size("lon")
    levels, width, nlat = lon_coeff.shape
    percol = width * nlat
    depth = VARS * LEV
    per_dev = obs_columns.shape[0]
    capacity = max(per_dev // 64, 2 * ((per_dev + devices - 1) // devices), 16)
    slots_all = devices * capacity
    bf16, f32 = jnp.bfloat16, jnp.float32

    lanes = -(-(depth + 4) // 128) * 128
    wide = 3 * width
    steps = (levels - 1).bit_length()
    rows = slots_all // nlat
    vmem = pl.BlockSpec(memory_space=pltpu.VMEM)
    far = pl.BlockSpec(memory_space=pltpu.HBM)
    own_shape = jax.ShapeDtypeStruct((width, depth, nlat), f32)
    last_shape = (2 * rows + 8, nlat)

    def held(*dims, dtype=f32):
        return pltpu.VMEM(dims, dtype)

    dma = pltpu.SemaphoreType.DMA
    control, increment, obs_fit = pl.pallas_call(
        loading_kernel,
        out_shape=[own_shape, own_shape, jax.ShapeDtypeStruct((1, per_dev), f32)],
        in_specs=[far] * 3 + [pl.BlockSpec(memory_space=pltpu.SMEM)] + [far] * 5,
        out_specs=[vmem] * 3,
        scratch_shapes=[
            held(3, width, levels, nlat),
            held(devices, capacity, lanes, dtype=bf16),
            held(devices, *last_shape),
            held(weight_table.shape[0], lanes, dtype=bf16),
            held(lanes, per_dev),
            held(3, width, levels, nlat),
            held(3, width, levels, nlat),
            held(devices, capacity, lanes, dtype=bf16),
            held(devices, capacity, lanes, dtype=bf16),
            held(devices, capacity, lanes, dtype=bf16),
            held(3, depth, slots_all, dtype=bf16),
            held(3, percol, slots_all, dtype=bf16),
            held(wide, levels, nlat),
            held(wide, levels, nlat),
            held(steps, wide, levels, nlat),
            held(steps, wide, levels, nlat),
            held(wide, levels, nlat),
            held(1, slots_all),
            held(wide, depth, nlat),
            held(width + 2 * STEPS, depth, nlat),
            held(width, depth, nlat),
            held(width, depth, nlat),
            held(width, depth, nlat),
            held(levels, nlat),
            held(levels, nlat),
            held(1, slots_all),
            held(1, slots_all),
            held(1, slots_all),
            held(8, nlat),
            held(devices, 8, nlat),
            held(*last_shape),
            dma((devices,)),
            dma((devices,)),
            dma((2, devices)),
            dma((2, devices)),
            dma((4,)),
            dma((4,)),
            dma((devices,)),
            dma((devices,)),
            dma((devices,)),
            dma((devices,)),
            held(1, per_dev),
            held(1, per_dev),
            held(1, per_dev, dtype=jnp.int32),
            held(1, per_dev, dtype=jnp.int32),
            held(*weight_table.shape, dtype=bf16),
            held(levels, width, nlat),
            held(levels, width, nlat),
            held(levels, width, nlat),
            dma((9,)),
        ],
        compiler_params=pltpu.CompilerParams(
            collective_id=0, has_side_effects=True, vmem_limit_bytes=48 * 2**20
        ),
    )(
        obs_departure.astype(f32).reshape(1, per_dev),
        obs_precision.astype(f32).reshape(1, per_dev),
        obs_columns.reshape(1, per_dev),
        obs_counts.reshape(1, 1),
        obs_blocks.reshape(1, per_dev),
        weight_table,
        lon_coeff,
        lat_coeff,
        vert_coeff,
    )

    def placed(field):
        return field.reshape(width, VARS, levels, nlat).transpose(1, 2, 0, 3)

    return placed(control), placed(increment), obs_fit.reshape(per_dev)


def solution(mesh):
    in_specs = (
        P(("member", "lon")),
        P("lon"),
        P("lon"),
        P("lon"),
        P("lon"),
        P("lon", None),
        P(None, "lon", None),
        P(None, "lon", None),
        P(None, "lon", None),
    )
    out_specs = (
        P("member", None, "lon", None),
        P("member", None, "lon", None),
        P(("member", "lon")),
    )
    return jax.shard_map(
        on_device, mesh=mesh, in_specs=in_specs, out_specs=out_specs, check_vma=False
    )
```
